32 devices in a mesh: blk: 8 (over y, x, core), head: 4 (over z).
Axes of the slice: x: 2, y: 2, z: 4, core: 2. Of those that a mesh axis runs over, the one named last changes fastest.
Arguments:
- queries: bfloat16 [4096, 2048], P(('blk', 'head')), may hold values from -6 to 6
- key_rows: bfloat16 [4096, 2048], P(('blk', 'head')), may hold values from -6 to 6
- value_rows: bfloat16 [4096, 2048], P(('blk', 'head')), may hold values from -6 to 6
- w_out: bfloat16 [2048, 2048], P('head'), may hold values from -0.125 to 0.125
- first_key: int32 [4096], P('blk'), may hold values from 0 to 4093, as said below
Outputs:
- mixed: bfloat16 [4096, 2048], P(('blk', 'head'))
The draws below stay inside these ranges and needn't reach their ends.
Inputs may be any that keep to these rules, and one draw needn't show every extreme that they name: first_key[i] <= max(i - 1, 0) and first_key[i] >= i - 512; the last bin of each aligned block of 512 bins has first_key exactly i - 512 where that is not negative; the next-to-last bin of the sequence has first_key exactly 4093.
All inputs are finite; a program needn't handle non-finite values.
Results may differ from the reference program's by a relative error of at most 0.0055.
Values may be sent and summed in bfloat16 or wider, within the bound.
A program may use at most 64 MiB of HBM per device.

```python
from functools import partial
import jax
import jax.numpy as jnp
from jax import lax

HEADS = 32
HEAD_DIM = 64
D = 2048
BLOCK_TOK = 512
SEQ = 4096
N_BLK = 8


def paired_fields(key):
    base = jax.random.fold_in(key, 11)
    key_query, key_keys = jax.random.split(base, 2)
    shape = (SEQ, HEADS, HEAD_DIM)
    query_field = jnp.clip(jax.random.normal(key_query, shape, jnp.float32), -6.0, 6.0)
    key_field = jnp.clip(jax.random.normal(key_keys, shape, jnp.float32), -6.0, 6.0)
    return (query_field.reshape(SEQ, D), key_field.reshape(SEQ, D))


def draw_queries(key, part):
    return paired_fields(key)[0].astype(jnp.bfloat16)


def draw_key_rows(key, part):
    return paired_fields(key)[1].astype(jnp.bfloat16)


def draw_first_key(key, part):
    base = jax.random.fold_in(key, 5)
    reach = jax.random.randint(base, (SEQ,), 1, BLOCK_TOK + 1, dtype=jnp.int32)
    position = jnp.arange(SEQ, dtype=jnp.int32)
    reach = jnp.where(position % BLOCK_TOK == BLOCK_TOK - 1, BLOCK_TOK, reach)
    reach = jnp.where(position == SEQ - 2, 1, reach)
    return jnp.maximum(position - reach, 0).astype(jnp.int32)


def block_levels(stream_key, dims, shards, low, high):
    factor_of = 1.0
    for axis_at, blocks in shards:
        draws = jax.random.uniform(jax.random.fold_in(jax.random.fold_in(stream_key, 6), axis_at), (blocks,), jnp.float32, low / len(shards), high / len(shards))
        factor_of = factor_of * jnp.repeat(jnp.exp(draws), dims[axis_at] // blocks).reshape((-1,) + (1,) * (len(dims) - 1 - axis_at))
    return factor_of


def centred(key, extent, width, limit, shards=(), kind=jnp.bfloat16):
    result = width * jax.random.normal(key, extent, jnp.float32)
    if shards:
        result = result * block_levels(key, extent, shards, -0.22, 0.18)
    return jnp.clip(result, -limit, limit).astype(kind)


def setup_inputs(seed: int = 0) -> dict:
    keys = jax.random.split(jax.random.key(seed), 6)
    queries = draw_queries(jax.random.fold_in(keys[5], 71), 0)
    key_rows = draw_key_rows(jax.random.fold_in(keys[5], 71), 0)
    value_rows = centred(keys[2], (SEQ, D), 1.0, 6.0, ((0, 32),))
    w_out = centred(keys[3], (D, D), D ** -0.5, 0.125, ((0, 4),))
    first_key = draw_first_key(jax.random.fold_in(keys[5], 71), 0)
    return {"queries": queries, "key_rows": key_rows, "value_rows": value_rows, "w_out": w_out, "first_key": first_key}


def attend(query_tile, key_tile, value_tile, lowest, query_pos, key_pos):
    scores = lax.dot_general(query_tile, key_tile, (((1,), (1,)), ((), ())), preferred_element_type=jnp.float32)
    scores = scores * (HEAD_DIM ** -0.5)
    allowed = (key_pos[None, :] >= lowest[:, None]) & (key_pos[None, :] <= query_pos[:, None])
    scores = jnp.where(allowed, scores, -jnp.inf)
    largest = jnp.max(scores, axis=1, keepdims=True)
    powers = jnp.exp(scores - largest)
    totals = jnp.sum(powers, axis=1, keepdims=True)
    weights = powers.astype(jnp.bfloat16)
    context = jnp.dot(weights, value_tile, preferred_element_type=jnp.float32) / totals
    return context.astype(jnp.bfloat16)


def head_block(queries, key_pad, value_pad, first_key, item):
    block_id = item // HEADS
    head_id = item % HEADS
    start = (block_id * BLOCK_TOK).astype(jnp.int32)
    column = (head_id * HEAD_DIM).astype(jnp.int32)
    query_tile = lax.dynamic_slice(queries, (start, column), (BLOCK_TOK, HEAD_DIM))
    key_tile = lax.dynamic_slice(key_pad, (start, column), (2 * BLOCK_TOK, HEAD_DIM))
    value_tile = lax.dynamic_slice(value_pad, (start, column), (2 * BLOCK_TOK, HEAD_DIM))
    lowest = lax.dynamic_slice_in_dim(first_key, start, BLOCK_TOK)
    query_pos = start + jnp.arange(BLOCK_TOK, dtype=jnp.int32)
    key_pos = start - BLOCK_TOK + jnp.arange(2 * BLOCK_TOK, dtype=jnp.int32)
    return attend(query_tile, key_tile, value_tile, lowest, query_pos, key_pos)


def reference(queries, key_rows, value_rows, w_out, first_key):
    padding = jnp.zeros((BLOCK_TOK, D), key_rows.dtype)
    key_pad = jnp.concatenate([padding, key_rows], axis=0)
    value_pad = jnp.concatenate([padding, value_rows], axis=0)
    items = jnp.arange(N_BLK * HEADS, dtype=jnp.int32)
    tiles = lax.map(partial(head_block, queries, key_pad, value_pad, first_key), items)
    context = tiles.reshape(N_BLK, HEADS, BLOCK_TOK, HEAD_DIM).transpose(0, 2, 1, 3).reshape(SEQ, D)
    return jnp.dot(context, w_out, preferred_element_type=jnp.float32).astype(jnp.bfloat16)
```

```python
import functools
import math

import jax
import jax.numpy as jnp
from jax import lax
from jax.experimental import pallas as pl
from jax.experimental.pallas import tpu as pltpu
from jax.sharding import PartitionSpec as P

HEAD_DIM = 64
PAIR = 2 * HEAD_DIM
MESH = pl.DeviceIdType.MESH
SCALE = HEAD_DIM ** (-0.5) * math.log2(math.e)


def kernel(
    n_blk, n_head, q_in, k_in, v_in, w_in, low_ref, out_ref,
    qb, kb, vb, vt, ctx, gathered, wb,
    own_sem, qkv_send, qkv_recv, halo_send, halo_recv, ctx_send, ctx_recv,
    w1_send, w1_recv, w2_send, w2_recv, w3_send, w3_recv,
):
    blk = lax.axis_index("blk")
    zed = lax.axis_index("head")
    rows, d_model = q_in.shape
    w_rows = w_in.shape[0]
    pairs, span, _ = qb.shape
    width = pairs * PAIR
    cols = n_blk // 2
    column, core = blk // 2, blk % 2
    piece = d_model // n_blk
    half = d_model // 2
    others = range(1, n_head)

    def ds(start, size, unit):
        return pl.ds(pl.multiple_of(start, unit), size)

    def remote(src, dst, send, recv, device):
        return pltpu.make_async_remote_copy(
            src_ref=src, dst_ref=dst, send_sem=send, recv_sem=recv,
            device_id=device, device_id_type=MESH,
        )

    def to_head(d):
        return lax.rem(zed + d, n_head)

    def from_head(d):
        return lax.rem(zed + n_head - d, n_head)

    streams = ((k_in, kb, span), (v_in, vb, span), (q_in, qb, 0))

    def lands(a, g):
        _, buf, base = streams[a]
        return buf.at[g, ds(base + zed * rows, rows, 128)]

    def exchange(a, g, d):
        src = streams[a][0].at[:, ds(to_head(d) * width + g * PAIR, PAIR, 128)]
        return remote(
            src, lands(a, g), qkv_send.at[a, g, d - 1], qkv_recv.at[a, g, d - 1],
            (blk, to_head(d)),
        )

    def own(a, g):
        src = streams[a][0].at[:, ds(zed * width + g * PAIR, PAIR, 128)]
        return pltpu.make_async_copy(src, lands(a, g), own_sem.at[a, g])

    def halo(a, g):
        buf = streams[a][1]
        return remote(
            buf.at[g, pl.ds(span, span)], buf.at[g, pl.ds(0, span)],
            halo_send.at[a, g], halo_recv.at[a, g],
            (lax.rem(blk + 1, n_blk), zed),
        )

    def give_back(g, d):
        return remote(
            ctx.at[g, ds(to_head(d) * rows, rows, 128)],
            gathered.at[zed, :, pl.ds(g * PAIR, PAIR)],
            ctx_send.at[g, d - 1], ctx_recv.at[g, d - 1],
            (blk, to_head(d)),
        )

    my_piece = ds(core * half + column * piece, piece, 128)

    def w_along_head(d):
        return remote(
            w_in.at[:, my_piece], wb.at[ds(zed * w_rows, w_rows, 128), my_piece],
            w1_send.at[d - 1], w1_recv.at[d - 1], (blk, to_head(d)),
        )

    def w_in_plane(d, e):
        part = wb.at[ds(from_head(d) * w_rows, w_rows, 128), my_piece]
        return remote(
            part, part, w2_send.at[d - 1, e - 1], w2_recv.at[d - 1, e - 1],
            (lax.rem(blk + 2 * e, n_blk), zed),
        )

    def w_to_sibling(d):
        part = wb.at[
            ds(from_head(d) * w_rows, w_rows, 128), ds(core * half, half, 128)
        ]
        return remote(
            part, part, w3_send.at[d - 1], w3_recv.at[d - 1],
            (blk + 1 - 2 * core, zed),
        )

    w_own = pltpu.make_async_copy(
        w_in, wb.at[ds(zed * w_rows, w_rows, 128)], own_sem.at[3, 0]
    )

    for g in range(pairs):
        for a in range(3):
            own(a, g).start()
    w_own.start()

    barrier = pltpu.get_barrier_semaphore()
    peers = [(blk, to_head(d)) for d in others]
    peers += [(lax.rem(blk + 2 * e, n_blk), zed) for e in range(1, cols)]
    peers += [(lax.rem(blk + 1, n_blk), zed), (lax.rem(blk + n_blk - 1, n_blk), zed)]
    for peer in peers:
        pl.semaphore_signal(barrier, inc=1, device_id=peer, device_id_type=MESH)
    pl.semaphore_wait(barrier, len(peers))

    for g in range(pairs):
        for a in range(3):
            for d in others:
                exchange(a, g, d).start()
        if g == 0:
            for d in others:
                w_along_head(d).start()

    def arrived(a, g):
        own(a, g).wait()
        for d in others:
            exchange(a, g, d).wait_recv()

    def tile(g, c):
        row0 = c * rows
        query = qb[g, ds(row0, rows, 128), :].astype(jnp.float32)
        lane = lax.broadcasted_iota(jnp.int32, (rows, PAIR), 1)
        both = jnp.concatenate(
            [jnp.where(lane < HEAD_DIM, query, 0.0), jnp.where(lane < HEAD_DIM, 0.0, query)], 0
        ).astype(jnp.bfloat16)
        contract = (((1,), (1,)), ((), ()))
        far = lax.dot_general(
            kb[g, ds(row0, span, 128), :], both, contract, preferred_element_type=jnp.float32
        )
        near = lax.dot_general(
            kb[g, ds(row0 + span, rows, 128), :], both, contract,
            preferred_element_type=jnp.float32,
        )
        low = low_ref[c] - (blk * span - span + row0)
        low = jnp.concatenate([low, low], 1)
        key_far = lax.broadcasted_iota(jnp.int32, (span, 2 * rows), 0)
        key_near = lax.broadcasted_iota(jnp.int32, (rows, 2 * rows), 0)
        bin_near = lax.broadcasted_iota(jnp.int32, (rows, 2 * rows), 1)
        bin_near = jnp.where(bin_near >= rows, bin_near - rows, bin_near)
        far = jnp.where(key_far >= low, far * SCALE, -jnp.inf)
        near = jnp.where(
            (key_near >= low - span) & (key_near <= bin_near), near * SCALE, -jnp.inf
        )
        largest = jnp.maximum(
            jnp.max(far, axis=0, keepdims=True), jnp.max(near, axis=0, keepdims=True)
        )
        far = jnp.exp2(far - largest)
        near = jnp.exp2(near - largest)
        totals = jnp.sum(far, axis=0, keepdims=True) + jnp.sum(near, axis=0, keepdims=True)
        mixed = jnp.dot(
            vt[:, ds(row0, span, 128)], far.astype(jnp.bfloat16),
            preferred_element_type=jnp.float32,
        ) + jnp.dot(
            vt[:, ds(row0 + span, rows, 128)], near.astype(jnp.bfloat16),
            preferred_element_type=jnp.float32,
        )
        mixed = mixed / totals
        mixed = jnp.concatenate([mixed[:HEAD_DIM, :rows], mixed[HEAD_DIM:, rows:]], 0)
        return mixed.T.astype(jnp.bfloat16)

    def attend(g):
        halo(0, g).wait_recv()
        halo(1, g).wait_recv()
        vt[...] = vb[g].T

        def step(t, carry):
            chunks = [lax.rem(zed + 1 + 2 * t + u, n_head) for u in range(2)]
            tiles = [tile(g, c) for c in chunks]
            for u in range(2):
                ctx[g, ds(chunks[u] * rows, rows, 128), :] = tiles[u]
            for u in range(2):
                d = 2 * t + u + 1

                @pl.when(d < n_head)
                def _():
                    give_back(g, d).start()

            return carry

        lax.fori_loop(0, n_head // 2, step, 0)
        gathered[zed, :, pl.ds(g * PAIR, PAIR)] = ctx[g, ds(zed * rows, rows, 128), :]

    for g in range(pairs):
        arrived(0, g)
        arrived(1, g)
        halo(0, g).start()
        halo(1, g).start()
        arrived(2, g)
        if g == min(1, pairs - 1):
            for d in others:
                w_along_head(d).wait_recv()
                for e in range(1, cols):
                    w_in_plane(d, e).start()
        if g >= 1:
            attend(g - 1)
    for d in others:
        for e in range(1, cols):
            w_in_plane(d, e).wait_recv()
        w_to_sibling(d).start()
    attend(pairs - 1)
    w_own.wait()
    for d in others:
        w_to_sibling(d).wait_recv()
    for g in range(pairs):
        for d in others:
            give_back(g, d).wait_recv()

    tile_n = 512
    for n in range(d_model // tile_n):
        col = pl.ds(n * tile_n, tile_n)
        total = jnp.zeros((rows, tile_n), jnp.float32)
        for s in range(n_head):
            total += jnp.dot(
                gathered[s], wb[pl.ds(s * w_rows, w_rows), col],
                preferred_element_type=jnp.float32,
            )
        out_ref[:, col] = total.astype(out_ref.dtype)

    for g in range(pairs):
        for a in range(3):
            for d in others:
                exchange(a, g, d).wait_send()
        halo(0, g).wait_send()
        halo(1, g).wait_send()
        for d in others:
            give_back(g, d).wait_send()
    for d in others:
        w_along_head(d).wait_send()
        for e in range(1, cols):
            w_in_plane(d, e).wait_send()
        w_to_sibling(d).wait_send()


def on_device(n_blk, n_head, queries, key_rows, value_rows, w_out, first_key):
    rows, d_model = queries.shape
    span = rows * n_head
    width = d_model // n_head
    pairs = width // PAIR
    cols = n_blk // 2
    low = first_key.reshape(n_head, 1, rows)
    bf16 = jnp.bfloat16
    dma = pltpu.SemaphoreType.DMA
    hbm = pl.BlockSpec(memory_space=pl.ANY)
    vmem = pl.BlockSpec(memory_space=pltpu.VMEM)
    return pl.pallas_call(
        functools.partial(kernel, n_blk, n_head),
        out_shape=jax.ShapeDtypeStruct((rows, d_model), bf16),
        in_specs=[hbm, hbm, hbm, hbm, vmem],
        out_specs=vmem,
        scratch_shapes=[
            pltpu.VMEM((pairs, span, PAIR), bf16),
            pltpu.VMEM((pairs, 2 * span, PAIR), bf16),
            pltpu.VMEM((pairs, 2 * span, PAIR), bf16),
            pltpu.VMEM((PAIR, 2 * span), bf16),
            pltpu.VMEM((pairs, span, PAIR), bf16),
            pltpu.VMEM((n_head, rows, width), bf16),
            pltpu.VMEM((d_model, d_model), bf16),
            dma((4, pairs)),
            dma((3, pairs, n_head - 1)), dma((3, pairs, n_head - 1)),
            dma((2, pairs)), dma((2, pairs)),
            dma((pairs, n_head - 1)), dma((pairs, n_head - 1)),
            dma((n_head - 1,)), dma((n_head - 1,)),
            dma((n_head - 1, cols - 1)), dma((n_head - 1, cols - 1)),
            dma((n_head - 1,)), dma((n_head - 1,)),
        ],
        compiler_params=pltpu.CompilerParams(
            collective_id=0, has_side_effects=True, vmem_limit_bytes=48 * 1024 * 1024
        ),
    )(queries, key_rows, value_rows, w_out, low)


def solution(mesh):
    placed = (
        P(("blk", "head"), None),
        P(("blk", "head"), None),
        P(("blk", "head"), None),
        P("head", None),
        P("blk"),
    )
    body = functools.partial(on_device, mesh.shape["blk"], mesh.shape["head"])
    return jax.shard_map(
        body, mesh=mesh, in_specs=placed, out_specs=P(("blk", "head"), None), check_vma=False
    )
```

```python
import functools
import math

import jax
import jax.numpy as jnp
from jax import lax
from jax.experimental import pallas as pl
from jax.experimental.pallas import tpu as pltpu
from jax.sharding import PartitionSpec as P

HEAD_DIM = 64
PAIR = 2 * HEAD_DIM
MESH = pl.DeviceIdType.MESH
SCALE = HEAD_DIM ** (-0.5) * math.log2(math.e)


def kernel(
    n_blk, n_head, q_in, k_in, v_in, w_in, low_ref, out_ref,
    qb, kb, vb, vt, ctx, gathered, wb, acc,
    own_sem, qkv_send, qkv_recv, halo_send, halo_recv, ctx_send, ctx_recv,
    w1_send, w1_recv, w2_send, w2_recv, w3_send, w3_recv,
):
    blk = lax.axis_index("blk")
    zed = lax.axis_index("head")
    rows, d_model = q_in.shape
    w_rows = w_in.shape[0]
    pairs, span, _ = qb.shape
    width = pairs * PAIR
    cols = n_blk // 2
    column, core = blk // 2, blk % 2
    piece = d_model // n_blk
    half = d_model // 2
    others = range(1, n_head)

    def ds(start, size, unit):
        return pl.ds(pl.multiple_of(start, unit), size)

    def remote(src, dst, send, recv, device):
        return pltpu.make_async_remote_copy(
            src_ref=src, dst_ref=dst, send_sem=send, recv_sem=recv,
            device_id=device, device_id_type=MESH,
        )

    def to_head(d):
        return lax.rem(zed + d, n_head)

    def from_head(d):
        return lax.rem(zed + n_head - d, n_head)

    streams = ((k_in, kb, span), (v_in, vb, span), (q_in, qb, 0))

    def lands(a, g):
        _, buf, base = streams[a]
        return buf.at[g, ds(base + zed * rows, rows, 128)]

    def exchange(a, g, d):
        src = streams[a][0].at[:, ds(to_head(d) * width + g * PAIR, PAIR, 128)]
        return remote(
            src, lands(a, g), qkv_send.at[a, g, d - 1], qkv_recv.at[a, g, d - 1],
            (blk, to_head(d)),
        )

    def own(a, g):
        src = streams[a][0].at[:, ds(zed * width + g * PAIR, PAIR, 128)]
        return pltpu.make_async_copy(src, lands(a, g), own_sem.at[a, g])

    def halo(a, g):
        buf = streams[a][1]
        return remote(
            buf.at[g, pl.ds(span, span)], buf.at[g, pl.ds(0, span)],
            halo_send.at[a, g], halo_recv.at[a, g],
            (lax.rem(blk + 1, n_blk), zed),
        )

    def give_back(g, d):
        return remote(
            ctx.at[g, ds(to_head(d) * rows, rows, 128)],
            gathered.at[zed, :, pl.ds(g * PAIR, PAIR)],
            ctx_send.at[g, d - 1], ctx_recv.at[g, d - 1],
            (blk, to_head(d)),
        )

    my_piece = ds(core * half + column * piece, piece, 128)

    def shard(s):
        return ds(s * w_rows, w_rows, 128)

    def w_hop(t, way):
        s = zed - way * (t - 1)
        part = wb.at[shard(s), my_piece]
        at = (max(0, -way), t - 1)
        return remote(
            w_in.at[:, my_piece] if t == 1 else part, part,
            w1_send.at[at], w1_recv.at[at], (blk, zed + way),
        )

    def hop_is_sent(t, way):
        s, to = zed - way * (t - 1), zed + way
        return (s >= 0) & (s < n_head) & (to >= 0) & (to < n_head)

    def hop_arrives(t, way):
        s = zed - way * t
        return (s >= 0) & (s < n_head)

    def w_got(t, way):
        s = zed - way * t
        part = wb.at[shard(s), my_piece]
        at = (max(0, -way), t - 1)
        return remote(part, part, w1_send.at[at], w1_recv.at[at], (blk, zed - way))

    def w_in_plane(s, e):
        part = wb.at[shard(s), my_piece]
        return remote(
            part, part, w2_send.at[s, e - 1], w2_recv.at[s, e - 1],
            (lax.rem(blk + 2 * e, n_blk), zed),
        )

    def w_to_sibling(s):
        part = wb.at[shard(s), ds(core * half, half, 128)]
        return remote(
            part, part, w3_send.at[s], w3_recv.at[s], (blk + 1 - 2 * core, zed),
        )

    def start_hop(t):
        for way in (1, -1):
            @pl.when(hop_is_sent(t, way))
            def _():
                w_hop(t, way).start()

    def take_hop(t):
        for way in (1, -1):
            @pl.when(hop_arrives(t, way))
            def _():
                w_got(t, way).wait_recv()
        if t < n_head - 1:
            start_hop(t + 1)
        for way in (1, -1):
            @pl.when(hop_arrives(t, way))
            def _():
                for e in range(1, cols):
                    w_in_plane(zed - way * t, e).start()

    w_own = pltpu.make_async_copy(
        w_in, wb.at[ds(zed * w_rows, w_rows, 128)], own_sem.at[3, 0]
    )

    for g in range(pairs):
        for a in range(3):
            own(a, g).start()
    w_own.start()

    barrier = pltpu.get_barrier_semaphore()
    peers = [(blk, to_head(d)) for d in others]
    peers += [(lax.rem(blk + 2 * e, n_blk), zed) for e in range(1, cols)]
    peers += [(lax.rem(blk + 1, n_blk), zed), (lax.rem(blk + n_blk - 1, n_blk), zed)]
    for peer in peers:
        pl.semaphore_signal(barrier, inc=1, device_id=peer, device_id_type=MESH)
    pl.semaphore_wait(barrier, len(peers))

    def send_pair(g):
        for a in range(3):
            for d in others:
                exchange(a, g, d).start()

    start_hop(1)
    for t in range(1, n_head):
        take_hop(t)
    for g in range(pairs):
        send_pair(g)

    def arrived(a, g):
        own(a, g).wait()
        for d in others:
            exchange(a, g, d).wait_recv()

    def tile(g, c):
        row0 = c * rows
        query = qb[g, ds(row0, rows, 128), :].astype(jnp.float32)
        lane = lax.broadcasted_iota(jnp.int32, (rows, PAIR), 1)
        both = jnp.concatenate(
            [jnp.where(lane < HEAD_DIM, query, 0.0), jnp.where(lane < HEAD_DIM, 0.0, query)], 0
        ).astype(jnp.bfloat16)
        contract = (((1,), (1,)), ((), ()))
        far = lax.dot_general(
            kb[g, ds(row0, span, 128), :], both, contract, preferred_element_type=jnp.float32
        )
        near = lax.dot_general(
            kb[g, ds(row0 + span, rows, 128), :], both, contract,
            preferred_element_type=jnp.float32,
        )
        low = low_ref[c] - (blk * span - span + row0)
        low = jnp.concatenate([low, low], 1)
        key_far = lax.broadcasted_iota(jnp.int32, (span, 2 * rows), 0)
        key_near = lax.broadcasted_iota(jnp.int32, (rows, 2 * rows), 0)
        bin_near = lax.broadcasted_iota(jnp.int32, (rows, 2 * rows), 1)
        bin_near = jnp.where(bin_near >= rows, bin_near - rows, bin_near)
        far = jnp.where(key_far >= low, far * SCALE, -jnp.inf)
        near = jnp.where(
            (key_near >= low - span) & (key_near <= bin_near), near * SCALE, -jnp.inf
        )
        largest = jnp.maximum(
            jnp.max(far, axis=0, keepdims=True), jnp.max(near, axis=0, keepdims=True)
        )
        far = jnp.exp2(far - largest)
        near = jnp.exp2(near - largest)
        totals = jnp.sum(far, axis=0, keepdims=True) + jnp.sum(near, axis=0, keepdims=True)
        mixed = jnp.dot(
            vt[:, ds(row0, span, 128)], far.astype(jnp.bfloat16),
            preferred_element_type=jnp.float32,
        ) + jnp.dot(
            vt[:, ds(row0 + span, rows, 128)], near.astype(jnp.bfloat16),
            preferred_element_type=jnp.float32,
        )
        mixed = mixed / totals
        mixed = jnp.concatenate([mixed[:HEAD_DIM, :rows], mixed[HEAD_DIM:, rows:]], 0)
        return mixed.T.astype(jnp.bfloat16)

    def attend(g):
        halo(0, g).wait_recv()
        halo(1, g).wait_recv()
        vt[...] = vb[g].T

        def step(t, carry):
            chunks = [lax.rem(zed + 1 + 2 * t + u, n_head) for u in range(2)]
            tiles = [tile(g, c) for c in chunks]
            for u in range(2):
                ctx[g, ds(chunks[u] * rows, rows, 128), :] = tiles[u]
            for u in range(2):
                d = 2 * t + u + 1

                @pl.when(d < n_head)
                def _():
                    give_back(g, d).start()

            return carry

        lax.fori_loop(0, n_head // 2, step, 0)
        gathered[zed, :, pl.ds(g * PAIR, PAIR)] = ctx[g, ds(zed * rows, rows, 128), :]

    for g in range(pairs):
        arrived(0, g)
        arrived(1, g)
        halo(0, g).start()
        halo(1, g).start()
        arrived(2, g)
        if g >= 1:
            attend(g - 1)
    for d in others:
        for e in range(1, cols):
            w_in_plane(from_head(d), e).wait_recv()
        w_to_sibling(from_head(d)).start()
    attend(pairs - 1)
    w_own.wait()
    for d in others:
        w_to_sibling(from_head(d)).wait_recv()
    tile_n = 512

    def project(first, last):
        for n in range(d_model // tile_n):
            col = pl.ds(n * tile_n, tile_n)
            total = jnp.zeros((rows, tile_n), jnp.float32) if first == 0 else acc[:, col]
            for s in range(n_head):
                total += jnp.dot(
                    gathered[s, :, first * PAIR:last * PAIR],
                    wb[s * w_rows + first * PAIR:s * w_rows + last * PAIR, col],
                    preferred_element_type=jnp.float32,
                )
            if last == pairs:
                out_ref[:, col] = total.astype(out_ref.dtype)
            else:
                acc[:, col] = total

    for g in range(pairs - 1):
        for d in others:
            give_back(g, d).wait_recv()
    if pairs > 1:
        project(0, pairs - 1)
    for d in others:
        give_back(pairs - 1, d).wait_recv()
    project(pairs - 1, pairs)

    for g in range(pairs):
        for a in range(3):
            for d in others:
                exchange(a, g, d).wait_send()
        halo(0, g).wait_send()
        halo(1, g).wait_send()
        for d in others:
            give_back(g, d).wait_send()
    for d in others:
        for way in (1, -1):
            @pl.when(hop_is_sent(d, way))
            def _():
                w_hop(d, way).wait_send()
        for e in range(1, cols):
            w_in_plane(from_head(d), e).wait_send()
        w_to_sibling(from_head(d)).wait_send()


def on_device(n_blk, n_head, queries, key_rows, value_rows, w_out, first_key):
    rows, d_model = queries.shape
    span = rows * n_head
    width = d_model // n_head
    pairs = width // PAIR
    cols = n_blk // 2
    low = first_key.reshape(n_head, 1, rows)
    bf16 = jnp.bfloat16
    dma = pltpu.SemaphoreType.DMA
    hbm = pl.BlockSpec(memory_space=pl.ANY)
    vmem = pl.BlockSpec(memory_space=pltpu.VMEM)
    return pl.pallas_call(
        functools.partial(kernel, n_blk, n_head),
        out_shape=jax.ShapeDtypeStruct((rows, d_model), bf16),
        in_specs=[hbm, hbm, hbm, hbm, vmem],
        out_specs=vmem,
        scratch_shapes=[
            pltpu.VMEM((pairs, span, PAIR), bf16),
            pltpu.VMEM((pairs, 2 * span, PAIR), bf16),
            pltpu.VMEM((pairs, 2 * span, PAIR), bf16),
            pltpu.VMEM((PAIR, 2 * span), bf16),
            pltpu.VMEM((pairs, span, PAIR), bf16),
            pltpu.VMEM((n_head, rows, width), bf16),
            pltpu.VMEM((d_model, d_model), bf16),
            pltpu.VMEM((rows, d_model), jnp.float32),
            dma((4, pairs)),
            dma((3, pairs, n_head - 1)), dma((3, pairs, n_head - 1)),
            dma((2, pairs)), dma((2, pairs)),
            dma((pairs, n_head - 1)), dma((pairs, n_head - 1)),
            dma((2, n_head - 1)), dma((2, n_head - 1)),
            dma((n_head, cols - 1)), dma((n_head, cols - 1)),
            dma((n_head,)), dma((n_head,)),
        ],
        compiler_params=pltpu.CompilerParams(
            collective_id=0, has_side_effects=True, vmem_limit_bytes=63 * 1024 * 1024
        ),
    )(queries, key_rows, value_rows, w_out, low)


def solution(mesh):
    placed = (
        P(("blk", "head"), None),
        P(("blk", "head"), None),
        P(("blk", "head"), None),
        P("head", None),
        P("blk"),
    )
    body = functools.partial(on_device, mesh.shape["blk"], mesh.shape["head"])
    return jax.shard_map(
        body, mesh=mesh, in_specs=placed, out_specs=P(("blk", "head"), None), check_vma=False
    )
```

```python
import functools
import math

import jax
import jax.numpy as jnp
from jax import lax
from jax.experimental import pallas as pl
from jax.experimental.pallas import tpu as pltpu
from jax.sharding import PartitionSpec as P

HEAD_DIM = 64
PAIR = 2 * HEAD_DIM
MESH = pl.DeviceIdType.MESH
SCALE = HEAD_DIM ** (-0.5) * math.log2(math.e)


def kernel(
    n_blk, n_head, q_in, k_in, v_in, w_in, low_ref, out_ref,
    qb, kb, vb, vt, ctx, gathered, wb, acc,
    own_sem, qkv_send, qkv_recv, halo_send, halo_recv, ctx_send, ctx_recv,
    w1_send, w1_recv, w2_send, w2_recv, w3_send, w3_recv,
):
    blk = lax.axis_index("blk")
    zed = lax.axis_index("head")
    rows, d_model = q_in.shape
    w_rows = w_in.shape[0]
    pairs, span, _ = qb.shape
    width = pairs * PAIR
    cols = n_blk // 2
    column, core = blk // 2, blk % 2
    piece = d_model // n_blk
    half = d_model // 2
    others = range(1, n_head)

    def ds(start, size, unit):
        return pl.ds(pl.multiple_of(start, unit), size)

    def remote(src, dst, send, recv, device):
        return pltpu.make_async_remote_copy(
            src_ref=src, dst_ref=dst, send_sem=send, recv_sem=recv,
            device_id=device, device_id_type=MESH,
        )

    def to_head(d):
        return lax.rem(zed + d, n_head)

    def from_head(d):
        return lax.rem(zed + n_head - d, n_head)

    streams = ((k_in, kb, span), (v_in, vb, span), (q_in, qb, 0))

    def lands(a, g):
        _, buf, base = streams[a]
        return buf.at[g, ds(base + zed * rows, rows, 128)]

    def exchange(a, g, d):
        src = streams[a][0].at[:, ds(to_head(d) * width + g * PAIR, PAIR, 128)]
        return remote(
            src, lands(a, g), qkv_send.at[a, g, d - 1], qkv_recv.at[a, g, d - 1],
            (blk, to_head(d)),
        )

    def own(a, g):
        src = streams[a][0].at[:, ds(zed * width + g * PAIR, PAIR, 128)]
        return pltpu.make_async_copy(src, lands(a, g), own_sem.at[a, g])

    def halo(a, g):
        buf = streams[a][1]
        return remote(
            buf.at[g, pl.ds(span, span)], buf.at[g, pl.ds(0, span)],
            halo_send.at[a, g], halo_recv.at[a, g],
            (lax.rem(blk + 1, n_blk), zed),
        )

    def give_back(g, d):
        return remote(
            ctx.at[g, ds(to_head(d) * rows, rows, 128)],
            gathered.at[zed, :, pl.ds(g * PAIR, PAIR)],
            ctx_send.at[g, d - 1], ctx_recv.at[g, d - 1],
            (blk, to_head(d)),
        )

    my_piece = ds(core * half + column * piece, piece, 128)

    def shard(s):
        return ds(s * w_rows, w_rows, 128)

    def w_hop(t, way):
        s = zed - way * (t - 1)
        part = wb.at[shard(s), my_piece]
        at = (max(0, -way), t - 1)
        return remote(
            w_in.at[:, my_piece] if t == 1 else part, part,
            w1_send.at[at], w1_recv.at[at], (blk, zed + way),
        )

    def hop_is_sent(t, way):
        s, to = zed - way * (t - 1), zed + way
        return (s >= 0) & (s < n_head) & (to >= 0) & (to < n_head)

    def hop_arrives(t, way):
        s = zed - way * t
        return (s >= 0) & (s < n_head)

    def w_got(t, way):
        s = zed - way * t
        part = wb.at[shard(s), my_piece]
        at = (max(0, -way), t - 1)
        return remote(part, part, w1_send.at[at], w1_recv.at[at], (blk, zed - way))

    def w_in_plane(s, e):
        part = wb.at[shard(s), my_piece]
        return remote(
            part, part, w2_send.at[s, e - 1], w2_recv.at[s, e - 1],
            (lax.rem(blk + 2 * e, n_blk), zed),
        )

    def w_to_sibling(s):
        part = wb.at[shard(s), ds(core * half, half, 128)]
        return remote(
            part, part, w3_send.at[s], w3_recv.at[s], (blk + 1 - 2 * core, zed),
        )

    def start_hop(t):
        for way in (1, -1):
            @pl.when(hop_is_sent(t, way))
            def _():
                w_hop(t, way).start()

    def take_hop(t):
        for way in (1, -1):
            @pl.when(hop_arrives(t, way))
            def _():
                w_got(t, way).wait_recv()
        if t < n_head - 1:
            start_hop(t + 1)
        for way in (1, -1):
            @pl.when(hop_arrives(t, way))
            def _():
                for e in range(1, cols):
                    w_in_plane(zed - way * t, e).start()

    w_own = pltpu.make_async_copy(
        w_in, wb.at[ds(zed * w_rows, w_rows, 128)], own_sem.at[3, 0]
    )

    for g in range(pairs):
        for a in range(3):
            own(a, g).start()
    w_own.start()

    barrier = pltpu.get_barrier_semaphore()
    peers = [(blk, to_head(d)) for d in others]
    peers += [(lax.rem(blk + 2 * e, n_blk), zed) for e in range(1, cols)]
    peers += [(lax.rem(blk + 1, n_blk), zed), (lax.rem(blk + n_blk - 1, n_blk), zed)]
    for peer in peers:
        pl.semaphore_signal(barrier, inc=1, device_id=peer, device_id_type=MESH)
    pl.semaphore_wait(barrier, len(peers))

    def send(arrays, g):
        for a in arrays:
            for d in sorted(others, key=lambda d: abs(d - n_head // 2)):
                exchange(a, g, d).start()

    start_hop(1)
    for t in range(1, n_head):
        if t == n_head - 1:
            send((0, 1), 0)
        take_hop(t)
    for g in range(1, pairs):
        send((0, 1), g)
        send((2,), g - 1)
    send((2,), pairs - 1)

    def arrived(a, g):
        own(a, g).wait()
        for d in others:
            exchange(a, g, d).wait_recv()

    def tile(g, c):
        row0 = c * rows
        query = qb[g, ds(row0, rows, 128), :].astype(jnp.float32)
        lane = lax.broadcasted_iota(jnp.int32, (rows, PAIR), 1)
        both = jnp.concatenate(
            [jnp.where(lane < HEAD_DIM, query, 0.0), jnp.where(lane < HEAD_DIM, 0.0, query)], 0
        ).astype(jnp.bfloat16)
        contract = (((1,), (1,)), ((), ()))
        far = lax.dot_general(
            kb[g, ds(row0, span, 128), :], both, contract, preferred_element_type=jnp.float32
        )
        near = lax.dot_general(
            kb[g, ds(row0 + span, rows, 128), :], both, contract,
            preferred_element_type=jnp.float32,
        )
        low = low_ref[c] - (blk * span - span + row0)
        low = jnp.concatenate([low, low], 1)
        key_far = lax.broadcasted_iota(jnp.int32, (span, 2 * rows), 0)
        key_near = lax.broadcasted_iota(jnp.int32, (rows, 2 * rows), 0)
        bin_near = lax.broadcasted_iota(jnp.int32, (rows, 2 * rows), 1)
        bin_near = jnp.where(bin_near >= rows, bin_near - rows, bin_near)
        far = jnp.where(key_far >= low, far * SCALE, -jnp.inf)
        near = jnp.where(
            (key_near >= low - span) & (key_near <= bin_near), near * SCALE, -jnp.inf
        )
        largest = jnp.maximum(
            jnp.max(far, axis=0, keepdims=True), jnp.max(near, axis=0, keepdims=True)
        )
        far = jnp.exp2(far - largest)
        near = jnp.exp2(near - largest)
        totals = jnp.sum(far, axis=0, keepdims=True) + jnp.sum(near, axis=0, keepdims=True)
        mixed = jnp.dot(
            vt[:, ds(row0, span, 128)], far.astype(jnp.bfloat16),
            preferred_element_type=jnp.float32,
        ) + jnp.dot(
            vt[:, ds(row0 + span, rows, 128)], near.astype(jnp.bfloat16),
            preferred_element_type=jnp.float32,
        )
        mixed = mixed / totals
        mixed = jnp.concatenate([mixed[:HEAD_DIM, :rows], mixed[HEAD_DIM:, rows:]], 0)
        return mixed.T.astype(jnp.bfloat16)

    def attend(g):
        halo(0, g).wait_recv()
        halo(1, g).wait_recv()
        vt[...] = vb[g].T

        def step(t, carry):
            chunks = [lax.rem(zed + 1 + 2 * t + u, n_head) for u in range(2)]
            tiles = [tile(g, c) for c in chunks]
            for u in range(2):
                ctx[g, ds(chunks[u] * rows, rows, 128), :] = tiles[u]
            for u in range(2):
                d = 2 * t + u + 1

                @pl.when(d < n_head)
                def _():
                    give_back(g, d).start()

            return carry

        lax.fori_loop(0, n_head // 2, step, 0)
        gathered[zed, :, pl.ds(g * PAIR, PAIR)] = ctx[g, ds(zed * rows, rows, 128), :]

    for g in range(pairs):
        arrived(0, g)
        arrived(1, g)
        halo(0, g).start()
        halo(1, g).start()
        if g >= 1:
            arrived(2, g - 1)
            attend(g - 1)
    for d in others:
        for e in range(1, cols):
            w_in_plane(from_head(d), e).wait_recv()
        w_to_sibling(from_head(d)).start()
    arrived(2, pairs - 1)
    attend(pairs - 1)
    w_own.wait()
    for d in others:
        w_to_sibling(from_head(d)).wait_recv()
    tile_n = 512

    def project(first, last):
        for n in range(d_model // tile_n):
            col = pl.ds(n * tile_n, tile_n)
            total = jnp.zeros((rows, tile_n), jnp.float32) if first == 0 else acc[:, col]
            for s in range(n_head):
                total += jnp.dot(
                    gathered[s, :, first * PAIR:last * PAIR],
                    wb[s * w_rows + first * PAIR:s * w_rows + last * PAIR, col],
                    preferred_element_type=jnp.float32,
                )
            if last == pairs:
                out_ref[:, col] = total.astype(out_ref.dtype)
            else:
                acc[:, col] = total

    for g in range(pairs - 1):
        for d in others:
            give_back(g, d).wait_recv()
    if pairs > 1:
        project(0, pairs - 1)
    for d in others:
        give_back(pairs - 1, d).wait_recv()
    project(pairs - 1, pairs)

    for g in range(pairs):
        for a in range(3):
            for d in others:
                exchange(a, g, d).wait_send()
        halo(0, g).wait_send()
        halo(1, g).wait_send()
        for d in others:
            give_back(g, d).wait_send()
    for d in others:
        for way in (1, -1):
            @pl.when(hop_is_sent(d, way))
            def _():
                w_hop(d, way).wait_send()
        for e in range(1, cols):
            w_in_plane(from_head(d), e).wait_send()
        w_to_sibling(from_head(d)).wait_send()


def on_device(n_blk, n_head, queries, key_rows, value_rows, w_out, first_key):
    rows, d_model = queries.shape
    span = rows * n_head
    width = d_model // n_head
    pairs = width // PAIR
    cols = n_blk // 2
    low = first_key.reshape(n_head, 1, rows)
    bf16 = jnp.bfloat16
    dma = pltpu.SemaphoreType.DMA
    hbm = pl.BlockSpec(memory_space=pl.ANY)
    vmem = pl.BlockSpec(memory_space=pltpu.VMEM)
    return pl.pallas_call(
        functools.partial(kernel, n_blk, n_head),
        out_shape=jax.ShapeDtypeStruct((rows, d_model), bf16),
        in_specs=[hbm, hbm, hbm, hbm, vmem],
        out_specs=vmem,
        scratch_shapes=[
            pltpu.VMEM((pairs, span, PAIR), bf16),
            pltpu.VMEM((pairs, 2 * span, PAIR), bf16),
            pltpu.VMEM((pairs, 2 * span, PAIR), bf16),
            pltpu.VMEM((PAIR, 2 * span), bf16),
            pltpu.VMEM((pairs, span, PAIR), bf16),
            pltpu.VMEM((n_head, rows, width), bf16),
            pltpu.VMEM((d_model, d_model), bf16),
            pltpu.VMEM((rows, d_model), jnp.float32),
            dma((4, pairs)),
            dma((3, pairs, n_head - 1)), dma((3, pairs, n_head - 1)),
            dma((2, pairs)), dma((2, pairs)),
            dma((pairs, n_head - 1)), dma((pairs, n_head - 1)),
            dma((2, n_head - 1)), dma((2, n_head - 1)),
            dma((n_head, cols - 1)), dma((n_head, cols - 1)),
            dma((n_head,)), dma((n_head,)),
        ],
        compiler_params=pltpu.CompilerParams(
            collective_id=0, has_side_effects=True, vmem_limit_bytes=63 * 1024 * 1024
        ),
    )(queries, key_rows, value_rows, w_out, low)


def solution(mesh):
    placed = (
        P(("blk", "head"), None),
        P(("blk", "head"), None),
        P(("blk", "head"), None),
        P("head", None),
        P("blk"),
    )
    body = functools.partial(on_device, mesh.shape["blk"], mesh.shape["head"])
    return jax.shard_map(
        body, mesh=mesh, in_specs=placed, out_specs=P(("blk", "head"), None), check_vma=False
    )
```

```python
import functools
import math

import jax
import jax.numpy as jnp
from jax import lax
from jax.experimental import pallas as pl
from jax.experimental.pallas import tpu as pltpu
from jax.sharding import PartitionSpec as P

HEAD_DIM = 64
PAIR = 2 * HEAD_DIM
MESH = pl.DeviceIdType.MESH
SCALE = HEAD_DIM ** (-0.5) * math.log2(math.e)


def kernel(
    n_blk, n_head, q_in, k_in, v_in, w_in, low_ref, out_ref,
    qb, kb, vb, vt, ctx, gathered, wb, acc,
    own_sem, qkv_send, qkv_recv, halo_send, halo_recv, ctx_send, ctx_recv,
    w1_send, w1_recv, w2_send, w2_recv, w3_send, w3_recv,
):
    blk = lax.axis_index("blk")
    zed = lax.axis_index("head")
    rows, d_model = q_in.shape
    w_rows = w_in.shape[0]
    pairs, span, _ = qb.shape
    width = pairs * PAIR
    cols = n_blk // 2
    column, core = blk // 2, blk % 2
    piece = d_model // n_blk
    half = d_model // 2
    others = range(1, n_head)

    def ds(start, size, unit):
        return pl.ds(pl.multiple_of(start, unit), size)

    def remote(src, dst, send, recv, device):
        return pltpu.make_async_remote_copy(
            src_ref=src, dst_ref=dst, send_sem=send, recv_sem=recv,
            device_id=device, device_id_type=MESH,
        )

    def to_head(d):
        return lax.rem(zed + d, n_head)

    def from_head(d):
        return lax.rem(zed + n_head - d, n_head)

    streams = ((k_in, kb, span), (v_in, vb, span), (q_in, qb, 0))

    def lands(a, g):
        _, buf, base = streams[a]
        return buf.at[g, ds(base + zed * rows, rows, 128)]

    def exchange(a, g, d):
        src = streams[a][0].at[:, ds(to_head(d) * width + g * PAIR, PAIR, 128)]
        return remote(
            src, lands(a, g), qkv_send.at[a, g, d - 1], qkv_recv.at[a, g, d - 1],
            (blk, to_head(d)),
        )

    def own(a, g):
        src = streams[a][0].at[:, ds(zed * width + g * PAIR, PAIR, 128)]
        return pltpu.make_async_copy(src, lands(a, g), own_sem.at[a, g])

    def halo(a, g):
        buf = streams[a][1]
        return remote(
            buf.at[g, pl.ds(span, span)], buf.at[g, pl.ds(0, span)],
            halo_send.at[a, g], halo_recv.at[a, g],
            (lax.rem(blk + 1, n_blk), zed),
        )

    def give_back(g, d):
        return remote(
            ctx.at[g, ds(to_head(d) * rows, rows, 128)],
            gathered.at[zed, :, pl.ds(g * PAIR, PAIR)],
            ctx_send.at[g, d - 1], ctx_recv.at[g, d - 1],
            (blk, to_head(d)),
        )

    my_piece = ds(core * half + column * piece, piece, 128)

    def shard(s):
        return ds(s * w_rows, w_rows, 128)

    def w_hop(t, way):
        s = zed - way * (t - 1)
        part = wb.at[shard(s), my_piece]
        at = (max(0, -way), t - 1)
        return remote(
            w_in.at[:, my_piece] if t == 1 else part, part,
            w1_send.at[at], w1_recv.at[at], (blk, zed + way),
        )

    def hop_is_sent(t, way):
        s, to = zed - way * (t - 1), zed + way
        return (s >= 0) & (s < n_head) & (to >= 0) & (to < n_head)

    def hop_arrives(t, way):
        s = zed - way * t
        return (s >= 0) & (s < n_head)

    def w_got(t, way):
        s = zed - way * t
        part = wb.at[shard(s), my_piece]
        at = (max(0, -way), t - 1)
        return remote(part, part, w1_send.at[at], w1_recv.at[at], (blk, zed - way))

    def w_in_plane(s, e):
        part = wb.at[shard(s), my_piece]
        return remote(
            part, part, w2_send.at[s, e - 1], w2_recv.at[s, e - 1],
            (lax.rem(blk + 2 * e, n_blk), zed),
        )

    def w_to_sibling(s):
        part = wb.at[shard(s), ds(core * half, half, 128)]
        return remote(
            part, part, w3_send.at[s], w3_recv.at[s], (blk + 1 - 2 * core, zed),
        )

    def start_hop(t):
        for way in (1, -1):
            @pl.when(hop_is_sent(t, way))
            def _():
                w_hop(t, way).start()

    def take_hop(t):
        for way in (1, -1):
            @pl.when(hop_arrives(t, way))
            def _():
                w_got(t, way).wait_recv()
        if t < n_head - 1:
            start_hop(t + 1)
        for way in (1, -1):
            @pl.when(hop_arrives(t, way))
            def _():
                for e in range(1, cols):
                    w_in_plane(zed - way * t, e).start()

    w_own = pltpu.make_async_copy(
        w_in, wb.at[ds(zed * w_rows, w_rows, 128)], own_sem.at[3, 0]
    )

    for g in range(pairs):
        for a in range(3):
            own(a, g).start()
    w_own.start()

    barrier = pltpu.get_barrier_semaphore()
    peers = [(blk, to_head(d)) for d in others]
    peers += [(lax.rem(blk + 2 * e, n_blk), zed) for e in range(1, cols)]
    peers += [(lax.rem(blk + 1, n_blk), zed), (lax.rem(blk + n_blk - 1, n_blk), zed)]
    for peer in peers:
        pl.semaphore_signal(barrier, inc=1, device_id=peer, device_id_type=MESH)
    pl.semaphore_wait(barrier, len(peers))

    def send(arrays, g):
        for a in arrays:
            for d in sorted(others, key=lambda d: abs(d - n_head // 2)):
                exchange(a, g, d).start()

    start_hop(1)
    for t in range(1, n_head):
        if t == max(1, n_head - 2):
            send((0,), 0)
        if t == n_head - 1:
            send((1,), 0)
        take_hop(t)
    for g in range(1, pairs):
        send((0, 1), g)
        send((2,), g - 1)
    send((2,), pairs - 1)

    def arrived(a, g):
        own(a, g).wait()
        for d in others:
            exchange(a, g, d).wait_recv()

    def tile(g, c):
        row0 = c * rows
        query = qb[g, ds(row0, rows, 128), :].astype(jnp.float32)
        lane = lax.broadcasted_iota(jnp.int32, (rows, PAIR), 1)
        both = jnp.concatenate(
            [jnp.where(lane < HEAD_DIM, query, 0.0), jnp.where(lane < HEAD_DIM, 0.0, query)], 0
        ).astype(jnp.bfloat16)
        contract = (((1,), (1,)), ((), ()))
        far = lax.dot_general(
            kb[g, ds(row0, span, 128), :], both, contract, preferred_element_type=jnp.float32
        )
        near = lax.dot_general(
            kb[g, ds(row0 + span, rows, 128), :], both, contract,
            preferred_element_type=jnp.float32,
        )
        low = low_ref[c] - (blk * span - span + row0)
        low = jnp.concatenate([low, low], 1)
        key_far = lax.broadcasted_iota(jnp.int32, (span, 2 * rows), 0)
        key_near = lax.broadcasted_iota(jnp.int32, (rows, 2 * rows), 0)
        bin_near = lax.broadcasted_iota(jnp.int32, (rows, 2 * rows), 1)
        bin_near = jnp.where(bin_near >= rows, bin_near - rows, bin_near)
        far = jnp.where(key_far >= low, far * SCALE, -jnp.inf)
        near = jnp.where(
            (key_near >= low - span) & (key_near <= bin_near), near * SCALE, -jnp.inf
        )
        largest = jnp.maximum(
            jnp.max(far, axis=0, keepdims=True), jnp.max(near, axis=0, keepdims=True)
        )
        far = jnp.exp2(far - largest)
        near = jnp.exp2(near - largest)
        totals = jnp.sum(far, axis=0, keepdims=True) + jnp.sum(near, axis=0, keepdims=True)
        mixed = jnp.dot(
            vt[:, ds(row0, span, 128)], far.astype(jnp.bfloat16),
            preferred_element_type=jnp.float32,
        ) + jnp.dot(
            vt[:, ds(row0 + span, rows, 128)], near.astype(jnp.bfloat16),
            preferred_element_type=jnp.float32,
        )
        mixed = mixed / totals
        mixed = jnp.concatenate([mixed[:HEAD_DIM, :rows], mixed[HEAD_DIM:, rows:]], 0)
        return mixed.T.astype(jnp.bfloat16)

    def attend(g):
        halo(0, g).wait_recv()
        halo(1, g).wait_recv()
        vt[...] = vb[g].T

        def step(t, carry):
            chunks = [lax.rem(zed + 1 + 2 * t + u, n_head) for u in range(2)]
            tiles = [tile(g, c) for c in chunks]
            for u in range(2):
                ctx[g, ds(chunks[u] * rows, rows, 128), :] = tiles[u]
            for u in range(2):
                d = 2 * t + u + 1

                @pl.when(d < n_head)
                def _():
                    give_back(g, d).start()

            return carry

        lax.fori_loop(0, n_head // 2, step, 0)
        gathered[zed, :, pl.ds(g * PAIR, PAIR)] = ctx[g, ds(zed * rows, rows, 128), :]

    for g in range(pairs):
        arrived(0, g)
        arrived(1, g)
        halo(0, g).start()
        halo(1, g).start()
        if g >= 1:
            arrived(2, g - 1)
            attend(g - 1)
    for d in others:
        for e in range(1, cols):
            w_in_plane(from_head(d), e).wait_recv()
        w_to_sibling(from_head(d)).start()
    arrived(2, pairs - 1)
    attend(pairs - 1)
    w_own.wait()
    for d in others:
        w_to_sibling(from_head(d)).wait_recv()
    tile_n = 512

    def project(first, last):
        for n in range(d_model // tile_n):
            col = pl.ds(n * tile_n, tile_n)
            total = jnp.zeros((rows, tile_n), jnp.float32) if first == 0 else acc[:, col]
            for s in range(n_head):
                total += jnp.dot(
                    gathered[s, :, first * PAIR:last * PAIR],
                    wb[s * w_rows + first * PAIR:s * w_rows + last * PAIR, col],
                    preferred_element_type=jnp.float32,
                )
            if last == pairs:
                out_ref[:, col] = total.astype(out_ref.dtype)
            else:
                acc[:, col] = total

    for g in range(pairs - 1):
        for d in others:
            give_back(g, d).wait_recv()
    if pairs > 1:
        project(0, pairs - 1)
    for d in others:
        give_back(pairs - 1, d).wait_recv()
    project(pairs - 1, pairs)

    for g in range(pairs):
        for a in range(3):
            for d in others:
                exchange(a, g, d).wait_send()
        halo(0, g).wait_send()
        halo(1, g).wait_send()
        for d in others:
            give_back(g, d).wait_send()
    for d in others:
        for way in (1, -1):
            @pl.when(hop_is_sent(d, way))
            def _():
                w_hop(d, way).wait_send()
        for e in range(1, cols):
            w_in_plane(from_head(d), e).wait_send()
        w_to_sibling(from_head(d)).wait_send()


def on_device(n_blk, n_head, queries, key_rows, value_rows, w_out, first_key):
    rows, d_model = queries.shape
    span = rows * n_head
    width = d_model // n_head
    pairs = width // PAIR
    cols = n_blk // 2
    low = first_key.reshape(n_head, 1, rows)
    bf16 = jnp.bfloat16
    dma = pltpu.SemaphoreType.DMA
    hbm = pl.BlockSpec(memory_space=pl.ANY)
    vmem = pl.BlockSpec(memory_space=pltpu.VMEM)
    return pl.pallas_call(
        functools.partial(kernel, n_blk, n_head),
        out_shape=jax.ShapeDtypeStruct((rows, d_model), bf16),
        in_specs=[hbm, hbm, hbm, hbm, vmem],
        out_specs=vmem,
        scratch_shapes=[
            pltpu.VMEM((pairs, span, PAIR), bf16),
            pltpu.VMEM((pairs, 2 * span, PAIR), bf16),
            pltpu.VMEM((pairs, 2 * span, PAIR), bf16),
            pltpu.VMEM((PAIR, 2 * span), bf16),
            pltpu.VMEM((pairs, span, PAIR), bf16),
            pltpu.VMEM((n_head, rows, width), bf16),
            pltpu.VMEM((d_model, d_model), bf16),
            pltpu.VMEM((rows, d_model), jnp.float32),
            dma((4, pairs)),
            dma((3, pairs, n_head - 1)), dma((3, pairs, n_head - 1)),
            dma((2, pairs)), dma((2, pairs)),
            dma((pairs, n_head - 1)), dma((pairs, n_head - 1)),
            dma((2, n_head - 1)), dma((2, n_head - 1)),
            dma((n_head, cols - 1)), dma((n_head, cols - 1)),
            dma((n_head,)), dma((n_head,)),
        ],
        compiler_params=pltpu.CompilerParams(
            collective_id=0, has_side_effects=True, vmem_limit_bytes=63 * 1024 * 1024
        ),
    )(queries, key_rows, value_rows, w_out, low)


def solution(mesh):
    placed = (
        P(("blk", "head"), None),
        P(("blk", "head"), None),
        P(("blk", "head"), None),
        P("head", None),
        P("blk"),
    )
    body = functools.partial(on_device, mesh.shape["blk"], mesh.shape["head"])
    return jax.shard_map(
        body, mesh=mesh, in_specs=placed, out_specs=P(("blk", "head"), None), check_vma=False
    )
```
